32 devices in a mesh: grp: 4 (over x, core), mem: 8 (over z, y).
Axes of the slice: x: 2, y: 2, z: 4, core: 2. Of those that a mesh axis runs over, the one named last changes fastest.
Arguments:
- amplitudes: bfloat16 [8, 8, 128, 2048], P('mem', 'grp'), may hold values from -6 to 6
- integrals: bfloat16 [8, 8, 2048, 2048], P('mem', 'grp'), may hold values from -0.0625 to 0.0625
- triples: int32 [4, 8, 12], P('grp', 'mem'), may hold values from -1 to 15, as said below
Outputs:
- residual: bfloat16 [8, 8, 128, 2048], P('grp', 'mem')
The draws below stay inside these ranges and needn't reach their ends.
Inputs may be any that keep to these rules, and one draw needn't show every extreme that they name: On each device the live codes are distinct, increasing, and stand before the empty slots; one device lists exactly 12 triples, the others 12, 6, 3 or 1.
All inputs are finite; a program needn't handle non-finite values.
Results may differ from the reference program's by a relative error of at most 0.001.
Values may be sent and summed in bfloat16 or wider, within the bound.
A program may use at most 128 MiB of HBM per device.

```python
import jax
import jax.numpy as jnp
from jax import lax

P_SIZE = 2048
ROWS = 128
VL = 1
NI = 8
NV = 8
CL = 2
K = 12
N_GRP = 4
N_MEM = 8


def draw_triples(key, part):
    key = jax.random.fold_in(key, 7)
    count_key, pick_key, full_key = jax.random.split(key, 3)
    devices_all = N_GRP * N_MEM
    dense = NI * VL * CL
    shifts = jax.random.randint(count_key, (devices_all,), 0, 4)
    counts = K // jnp.left_shift(jnp.ones((devices_all,), jnp.int32), shifts)
    fullest = jax.random.randint(full_key, (), 0, devices_all)
    counts = jnp.where(jnp.arange(devices_all) == fullest, K, counts)
    keys = jax.random.split(pick_key, devices_all)

    def one_device(device_key, count):
        chosen = jax.random.permutation(device_key, dense)[:K]
        slots = jnp.arange(K, dtype=jnp.int32)
        scores = jnp.where(slots < count, chosen, dense + slots)
        ordered = jnp.sort(scores)
        return jnp.where(ordered < dense, ordered, -1).astype(jnp.int32)
    listed = jax.vmap(one_device)(keys, counts)
    return listed.reshape(N_GRP, N_MEM, K)


def block_levels(key, extent, shards, least, high):
    def one(axis_at, blocks):
        steps = jax.random.uniform(jax.random.fold_in(jax.random.fold_in(key, 6), axis_at), (blocks,), jnp.float32, least / len(shards), high / len(shards))
        return jnp.repeat(jnp.exp(steps), extent[axis_at] // blocks).reshape((-1,) + (1,) * (len(extent) - axis_at - 1))

    gain = one(*shards[0])
    for cut in shards[1:]:
        gain = gain * one(*cut)
    return gain


def normal_values(stream_key, dims, scale, limit, pieces=(), kind=jnp.bfloat16):
    result = jax.random.normal(stream_key, dims, jnp.float32) * scale
    if len(pieces) > 0:
        result = block_levels(stream_key, dims, pieces, -0.22, 0.18) * result
    return jnp.clip(result, min=-limit, max=limit).astype(kind)


def setup_inputs(seed: int = 0) -> dict:
    arg_keys = jax.random.split(jax.random.key(seed), 4)
    amplitudes = normal_values(arg_keys[0], (NI, NV, ROWS, P_SIZE), 1.0, 6.0, ((0, 8), (1, 4)))
    integrals = normal_values(arg_keys[1], (NV, NV, P_SIZE, P_SIZE), (P_SIZE * NV // 2) ** -0.5, 0.0625, ((0, 8), (1, 4)))
    triples = draw_triples(jax.random.fold_in(arg_keys[3], 71), 0)
    return {"amplitudes": amplitudes, "integrals": integrals, "triples": triples}


def reference(amplitudes, integrals, triples):
    rows = amplitudes.shape[2]
    width = amplitudes.shape[3]
    pairs = VL * CL
    table = triples.reshape(N_GRP * N_MEM, K)

    def device_terms(index, total):
        group = index // N_MEM
        member = index % N_MEM
        codes = table[index]
        live = (codes >= 0).astype(jnp.float32)
        safe = jnp.maximum(codes, 0)
        occ_tile = (safe // pairs).astype(jnp.int32)
        ab_tile = ((safe % pairs) // CL + member * VL).astype(jnp.int32)
        cd_tile = (safe % CL + group * CL).astype(jnp.int32)

        def one_triple(slot, inner):
            left = amplitudes[occ_tile[slot], cd_tile[slot]].astype(jnp.float32)
            right = integrals[ab_tile[slot], cd_tile[slot]].astype(jnp.float32)
            product = jnp.dot(left, right.T, preferred_element_type=jnp.float32) * live[slot]
            return inner.at[occ_tile[slot], ab_tile[slot]].add(product)

        return lax.fori_loop(0, K, one_triple, total)

    start = jnp.zeros((NI, NV, rows, width), jnp.float32)
    total = lax.fori_loop(0, N_GRP * N_MEM, device_terms, start)
    return total.astype(jnp.bfloat16)
```

```python
import functools

import jax
import jax.numpy as jnp
from jax import lax
from jax.experimental import pallas as pl
from jax.experimental.pallas import tpu as pltpu
from jax.sharding import PartitionSpec as P

MESH = pl.DeviceIdType.MESH
LINE = 4
HALVES = 2

ORDERS = (
    "0a 0b 1a 0A 1b 0B 2a 1A 2b 2A 3a 2B 3b 3A 3B 1B",
    "1a 1b 2a 0a 1A 2b 0b 2A 3a 2B 3b 1B 3A 3B 0A 0B",
    "2a 2b 3a 1a 2A 3b 1b 0a 3A 3B 0b 2B 1A 1B 0A 0B",
    "3a 3b 2a 3A 2b 3B 1a 2A 1b 0a 1A 0b 1B 0A 2B 0B",
)


def entries(order):
    return [(int(s[0]), int(s[1].isupper()), "ab".index(s[1].lower())) for s in order.split()]


def tables():
    out = []
    for x in range(2):
        for z in range(LINE):
            steps = entries(ORDERS[z if x == 0 else LINE - 1 - z])
            out.append([(sz if x == 0 else LINE - 1 - sz) * 4 + oy * 2 + h for sz, oy, h in steps])
    return out


def ladder_kernel(mask_ref, amp_ref, int_ref, out_ref, held, ints, part, near, far,
                  load_sem, ints_sem, get_sem, up_sem, down_sem, side_sem,
                  core_send, core_get, far_send, far_get):
    grp, mem = lax.axis_index("grp"), lax.axis_index("mem")
    x, core = grp // 2, grp % 2
    z, y = mem // 2, mem % 2
    up, down, side = {"mem": mem + 2}, {"mem": mem - 2}, {"mem": z * 2 + 1 - y}
    pair_z = z + 1 - 2 * (z % 2)
    pair = {"mem": pair_z * 2 + y}
    twin = {"grp": x * 2 + 1 - core}
    across = {"grp": (1 - x) * 2 + core}
    width = ints.shape[1]
    rows = held.shape[2]

    load = pltpu.make_async_copy(amp_ref.at[0], held.at[mem], load_sem)
    load.start()
    fetch = [pltpu.make_async_copy(int_ref.at[0, h], ints.at[h], ints_sem.at[h]) for h in range(HALVES)]
    for copy in fetch:
        copy.start()

    barrier = pltpu.get_barrier_semaphore()
    for neighbour in (side, twin, across):
        pl.semaphore_signal(barrier, inc=1, device_id=neighbour, device_id_type=MESH)

    @pl.when(z < LINE - 1)
    def _():
        pl.semaphore_signal(barrier, inc=1, device_id=up, device_id_type=MESH)

    @pl.when(z > 0)
    def _():
        pl.semaphore_signal(barrier, inc=1, device_id=down, device_id_type=MESH)

    @pl.when((z > 0) & (z < LINE - 1))
    def _():
        pl.semaphore_wait(barrier, 5)

    @pl.when((z == 0) | (z == LINE - 1))
    def _():
        pl.semaphore_wait(barrier, 4)

    load.wait()

    def push(tile, half, sems, target):
        return pltpu.make_async_remote_copy(
            src_ref=held.at[tile, half], dst_ref=held.at[tile, half],
            send_sem=sems.at[tile, half], recv_sem=get_sem.at[tile, half],
            device_id=target, device_id_type=MESH,
        )

    def pushes(sz, other, half, act):
        tile = sz * 2 + y + other - 2 * y * other
        same = other == 0

        @pl.when(same & (sz <= z) & (z < LINE - 1))
        def _():
            act(push(tile, half, up_sem, up))

        @pl.when(same & (sz >= z) & (z > 0))
        def _():
            act(push(tile, half, down_sem, down))

        @pl.when(same & ((sz != pair_z) | (half == 0)))
        def _():
            act(push(tile, half, side_sem, side))

        @pl.when((other == 1) & (sz == z) & (half == 1))
        def _():
            act(push(tile, half, up_sem, pair))

    for half in range(HALVES):
        pushes(z, 0, half, lambda copy: copy.start())

    part[...] = jnp.zeros_like(part)
    for copy in fetch:
        copy.wait()

    codes = tables()
    words = []
    for base in range(0, 16, 4):
        word = jnp.int32(0)
        for place, steps in enumerate(codes):
            packed = sum(c << (4 * i) for i, c in enumerate(steps[base:base + 4]))
            word = jnp.where(x * LINE + z == place, packed, word)
        words.append(word)

    def entry(step):
        word = words[0]
        for i in range(1, 4):
            word = jnp.where(step // 4 == i, words[i], word)
        shift = step % 4
        scale = jnp.where(shift == 0, 1, jnp.where(shift == 1, 16, jnp.where(shift == 2, 256, 4096)))
        code = word // scale % 16
        return code // 4, code // 2 % 2, code % 2

    def to_twin(tile):
        place = tile // 4 * 2 + tile % 2
        return pltpu.make_async_remote_copy(
            src_ref=part.at[tile], dst_ref=near.at[place],
            send_sem=core_send.at[place], recv_sem=core_get.at[place],
            device_id=twin, device_id_type=MESH,
        )

    def to_across(tile):
        place = tile % 2
        return pltpu.make_async_remote_copy(
            src_ref=part.at[tile], dst_ref=far.at[place],
            send_sem=far_send.at[place], recv_sem=far_get.at[place],
            device_id=across, device_id_type=MESH,
        )

    def one_step(step, carry):
        sz, other, half = entry(step)
        tile = sz * 2 + y + other - 2 * y * other

        @pl.when(step >= HALVES)
        def _():
            push(tile, half, up_sem, pair).wait_recv()
            pushes(sz, other, half, lambda copy: copy.start())

        scale = mask_ref[tile * 2 + half]

        def columns(n, inner):
            at = pl.ds(pl.multiple_of(n * 512, 512), 512)
            product = lax.dot_general(
                held[tile, half], ints[half, at, :], (((1,), (1,)), ((), ())),
                preferred_element_type=jnp.float32,
            )
            part[tile, :, at] += product * scale
            return inner

        lax.fori_loop(0, width // 512, columns, 0)
        mine = tile // 2 % 2 == core

        @pl.when((half == 1) & jnp.logical_not(mine))
        def _():
            to_twin(tile).start()

        @pl.when((half == 1) & mine & (tile // 4 != x))
        def _():
            to_twin(tile).wait_recv()
            part[tile] += near[tile // 4 * 2 + tile % 2]
            to_across(tile).start()

        return carry

    lax.fori_loop(0, 16, one_step, 0)

    for k in range(2):
        tile = grp * 2 + k
        to_twin(tile).wait_recv()
        kept = part[tile] + near[x * 2 + k]
        to_across(tile).wait_recv()
        out_ref[k, 0] = (kept + far[k]).astype(out_ref.dtype)

    def settle(step, carry):
        sz, other, half = entry(step)
        pushes(sz, other, half, lambda copy: copy.wait_send())
        return carry

    lax.fori_loop(0, 16, settle, 0)
    for place in range(4):
        tile = place // 2 * 4 + (1 - core) * 2 + place % 2
        to_twin(tile).wait_send()
    for k in range(2):
        to_across((1 - x) * 4 + core * 2 + k).wait_send()


def fused_body(amplitudes, integrals, triples):
    rows, width = amplitudes.shape[2:]
    codes = triples.reshape(-1)
    tiles = 8
    listed = (codes[None, :] == jnp.arange(tiles * HALVES, dtype=jnp.int32)[:, None]).any(axis=1)
    flops = 2 * tiles * HALVES * rows * width * width
    return pl.pallas_call(
        ladder_kernel,
        out_shape=jax.ShapeDtypeStruct((2, 1, rows, width), jnp.bfloat16),
        in_specs=[
            pl.BlockSpec(memory_space=pltpu.SMEM),
            pl.BlockSpec(memory_space=pl.ANY),
            pl.BlockSpec(memory_space=pl.ANY),
        ],
        out_specs=pl.BlockSpec(memory_space=pltpu.VMEM),
        scratch_shapes=[
            pltpu.VMEM((tiles, HALVES, rows, width), jnp.bfloat16),
            pltpu.VMEM((HALVES, width, width), jnp.bfloat16),
            pltpu.VMEM((tiles, rows, width), jnp.float32),
            pltpu.VMEM((4, rows, width), jnp.float32),
            pltpu.VMEM((2, rows, width), jnp.float32),
            pltpu.SemaphoreType.DMA,
            pltpu.SemaphoreType.DMA((HALVES,)),
            pltpu.SemaphoreType.DMA((tiles, HALVES)),
            pltpu.SemaphoreType.DMA((tiles, HALVES)),
            pltpu.SemaphoreType.DMA((tiles, HALVES)),
            pltpu.SemaphoreType.DMA((tiles, HALVES)),
            pltpu.SemaphoreType.DMA((4,)),
            pltpu.SemaphoreType.DMA((4,)),
            pltpu.SemaphoreType.DMA((2,)),
            pltpu.SemaphoreType.DMA((2,)),
        ],
        compiler_params=pltpu.CompilerParams(
            collective_id=0, has_side_effects=True, vmem_limit_bytes=56 * 2**20,
        ),
        cost_estimate=pl.CostEstimate(flops=flops, bytes_accessed=18 * 2**20, transcendentals=0),
    )(listed.astype(jnp.float32), amplitudes, integrals)


def body(amplitudes, integrals, triples):
    occ_local, cd_local, rows, width = amplitudes.shape
    ab_local = integrals.shape[0]
    gathered = lax.all_gather(amplitudes, "mem", axis=0, tiled=True)
    occ_tiles = gathered.shape[0]
    pairs = ab_local * cd_local
    codes = triples.reshape(-1)
    capacity = codes.shape[0]
    live = codes >= 0
    safe = jnp.maximum(codes, 0)
    occ_index = jnp.where(live, safe // pairs, occ_tiles)
    ab_index = safe % pairs // cd_local
    cd_index = safe % cd_local
    amp_flat = gathered.reshape(occ_tiles * cd_local, rows, width)
    int_flat = integrals.reshape(pairs, width, width)
    live_count = jnp.sum(live.astype(jnp.int32))
    empty = jnp.zeros((occ_tiles * ab_local, rows, width), jnp.float32)

    def one_triple(slot, total):
        place = jnp.minimum(slot, capacity - 1)
        occ = occ_index[place]
        outer = ab_index[place]
        inner = cd_index[place]
        left = lax.dynamic_index_in_dim(amp_flat, occ * cd_local + inner, 0, keepdims=False)
        right = lax.dynamic_index_in_dim(int_flat, outer * cd_local + inner, 0, keepdims=False)
        product = lax.dot_general(
            left, right, (((1,), (1,)), ((), ())), preferred_element_type=jnp.float32
        )
        target_row = (occ - 0) * ab_local + outer
        current = lax.dynamic_index_in_dim(total, target_row, 0, keepdims=False)
        return lax.dynamic_update_index_in_dim(total, current + product, target_row, 0)

    partial_value = lax.fori_loop(0, live_count, one_triple, empty)
    summed = lax.psum_scatter(
        partial_value.reshape(occ_tiles, ab_local, rows, width),
        "grp",
        scatter_dimension=0,
        tiled=True,
    )
    return summed.astype(jnp.bfloat16)


def solution(mesh):
    small = (mesh.shape["grp"], mesh.shape["mem"]) == (4, 8)
    return jax.shard_map(
        fused_body if small else body,
        mesh=mesh,
        in_specs=(P("mem", "grp", None, None), P("mem", "grp", None, None), P("grp", "mem", None)),
        out_specs=P("grp", "mem", None, None),
        check_vma=False,
    )
```

```python
import functools

import jax
import jax.numpy as jnp
from jax import lax
from jax.experimental import pallas as pl
from jax.experimental.pallas import tpu as pltpu
from jax.sharding import PartitionSpec as P

MESH = pl.DeviceIdType.MESH
LINE = 4
HALVES = 2
PARTS = 2

FIRST_SENDS = 5
MAIN_EVENTS = 114
EVENTS = (
    (
        8700960, 25183331, 25446016, 2100386, 10093760, 35131911, 35784385, 4196391, 67208304, 29630981,
        67471012, 4728976, 71404658, 30156309, 71667378, 6302868, 6169720, 47772185, 7418131, 73462810,
        32257565, 73757800, 7918236, 8270858, 74273803, 3676350, 3939080, 45748876, 75645216, 75645216,
        75645216, 75645216, 75645216, 75645216, 75645216, 75645216, 75645216, 75645216, 75645216,
    ),
    (
        27824168, 28086825, 11341866, 3670186, 29401104, 69849288, 3932704, 29663761, 61182592, 8723723,
        5244048, 29926418, 71426250, 5506594, 30189075, 63280802, 9266449, 5770388, 31502360, 71951552,
        6565383, 35189337, 72214209, 7418038, 32027674, 73527490, 23868957, 27300987, 65373882, 19740953,
        65551465, 25206042, 65895455, 25468699, 69325836, 61691917, 62392585, 42994432, 75629295,
    ),
    (
        29925424, 30188081, 29402162, 21784208, 2188401, 54538262, 14296304, 2420824, 35664407, 72213201,
        23359126, 2699385, 55063572, 23732466, 7088651, 63809194, 23947537, 7340218, 25182238, 73527510,
        8141313, 33604129, 73790167, 621724, 25707524, 67237056, 9177603, 27283555, 65897122, 10815745,
        50859113, 27809026, 51203079, 28071683, 69308428, 52762637, 52960521, 45621002, 75634379,
    ),
    (
        23393368, 39892091, 4289627, 65069086, 4504858, 31515167, 74314384, 31768222, 65546258, 5515024,
        71694002, 7351444, 6172926, 66939933, 96537, 25428576, 67111040, 1360898, 918148, 1655907, 27267330,
        67980295, 35705353, 2756620, 36706922, 28055305, 69737642, 75586575, 75645216, 75645216, 75645216,
        75645216, 75645216, 75645216, 75645216, 75645216, 75645216, 75645216, 75645195,
    ),
)


def ladder_kernel(mask_ref, amp_ref, int_ref, out_ref, held, ints, part, near, far,
                  load_sem, ints_sem, get_sem, up_sem, down_sem, side_sem,
                  core_send, core_get, far_send, far_get):
    grp, mem = lax.axis_index("grp"), lax.axis_index("mem")
    x, core = grp // 2, grp % 2
    z, y = mem // 2, mem % 2
    place_z = z + x * (LINE - 1 - 2 * z)
    toward = 2 - 4 * x
    up, down, side = {"mem": mem + toward}, {"mem": mem - toward}, {"mem": z * 2 + 1 - y}
    twin = {"grp": x * 2 + 1 - core}
    across = {"grp": (1 - x) * 2 + core}
    width = ints.shape[1]
    rows = held.shape[2]

    load = pltpu.make_async_copy(amp_ref.at[0], held.at[mem], load_sem)
    load.start()
    fetch = [pltpu.make_async_copy(int_ref.at[0, h], ints.at[h], ints_sem.at[h]) for h in range(HALVES)]
    for copy in fetch:
        copy.start()

    barrier = pltpu.get_barrier_semaphore()
    for neighbour in (side, twin, across):
        pl.semaphore_signal(barrier, inc=1, device_id=neighbour, device_id_type=MESH)

    @pl.when(place_z < LINE - 1)
    def _():
        pl.semaphore_signal(barrier, inc=1, device_id=up, device_id_type=MESH)

    @pl.when(place_z > 0)
    def _():
        pl.semaphore_signal(barrier, inc=1, device_id=down, device_id_type=MESH)

    @pl.when((z > 0) & (z < LINE - 1))
    def _():
        pl.semaphore_wait(barrier, 5)

    @pl.when((z == 0) | (z == LINE - 1))
    def _():
        pl.semaphore_wait(barrier, 4)

    load.wait()

    share = rows // PARTS

    def push(tile, half, piece, sems, target):
        at = pl.ds(pl.multiple_of(piece * share, share), share)
        return pltpu.make_async_remote_copy(
            src_ref=held.at[tile, half, at], dst_ref=held.at[tile, half, at],
            send_sem=sems.at[tile, half * PARTS + piece], recv_sem=get_sem.at[tile, half * PARTS + piece],
            device_id=target, device_id_type=MESH,
        )

    words = []
    for choices in zip(*EVENTS):
        word = jnp.int32(choices[0])
        for i in range(1, LINE):
            word = jnp.where(place_z == i, choices[i], word)
        words.append(word)

    def event(step):
        word = words[0]
        for i in range(1, len(words)):
            word = jnp.where(step // 3 == i, words[i], word)
        third = step % 3
        code = word // jnp.where(third == 0, 1, jnp.where(third == 1, 512, 512 * 512)) % 512
        sz = code // 8 % 4
        sz = sz + x * (LINE - 1 - 2 * sz)
        other = code // 4 % 2
        tile = sz * 2 + y + other - 2 * y * other
        return code // 32, tile, code // 2 % 2, code % 2

    ways = ((up_sem, up), (down_sem, down), (side_sem, side))

    def to_twin(tile):
        place = tile // 4 * 2 + tile % 2
        return pltpu.make_async_remote_copy(
            src_ref=part.at[tile], dst_ref=near.at[place],
            send_sem=core_send.at[place], recv_sem=core_get.at[place],
            device_id=twin, device_id_type=MESH,
        )

    def to_across(tile):
        place = tile % 2
        return pltpu.make_async_remote_copy(
            src_ref=part.at[tile], dst_ref=far.at[place],
            send_sem=far_send.at[place], recv_sem=far_get.at[place],
            device_id=across, device_id_type=MESH,
        )

    def multiply(tile, half):
        scale = mask_ref[tile * 2 + half]

        def columns(n, inner):
            at = pl.ds(pl.multiple_of(n * 512, 512), 512)
            product = lax.dot_general(
                ints[half, at, :], held[tile, half], (((1,), (1,)), ((), ())),
                preferred_element_type=jnp.float32,
            )
            part[tile, at, :] += product * scale
            return inner

        lax.fori_loop(0, width // 512, columns, 0)

    def one_event(step, carry):
        kind, tile, half, piece = event(step)

        @pl.when(kind == 0)
        def _():
            push(tile, half, piece, side_sem, side).wait_recv()

        for i, (sems, target) in enumerate(ways):
            @pl.when(kind == 1 + i)
            def _():
                push(tile, half, piece, sems, target).start()

            @pl.when(kind == 6 + i)
            def _():
                push(tile, half, piece, sems, target).wait_send()

        @pl.when((kind == 4) | (kind == 5))
        def _():
            multiply(tile, half)

        mine = tile // 2 % 2 == core

        @pl.when((kind == 5) & jnp.logical_not(mine))
        def _():
            to_twin(tile).start()

        @pl.when((kind == 5) & mine & (tile // 4 != x))
        def _():
            to_twin(tile).wait_recv()
            part[tile] += near[tile // 4 * 2 + tile % 2]
            to_across(tile).start()

        return carry

    lax.fori_loop(0, FIRST_SENDS, one_event, 0)
    part[...] = jnp.zeros_like(part)
    for copy in fetch:
        copy.wait()

    lax.fori_loop(FIRST_SENDS, MAIN_EVENTS, one_event, 0)

    for k in range(2):
        tile = grp * 2 + k
        to_twin(tile).wait_recv()
        kept = part[tile] + near[x * 2 + k]
        to_across(tile).wait_recv()
        out_ref[k, 0] = (kept + far[k]).T.astype(out_ref.dtype)

    lax.fori_loop(MAIN_EVENTS, 3 * len(words), one_event, 0)
    for place in range(4):
        tile = place // 2 * 4 + (1 - core) * 2 + place % 2
        to_twin(tile).wait_send()
    for k in range(2):
        to_across((1 - x) * 4 + core * 2 + k).wait_send()


def fused_body(amplitudes, integrals, triples):
    rows, width = amplitudes.shape[2:]
    codes = triples.reshape(-1)
    tiles = 8
    listed = (codes[None, :] == jnp.arange(tiles * HALVES, dtype=jnp.int32)[:, None]).any(axis=1)
    flops = 2 * tiles * HALVES * rows * width * width
    return pl.pallas_call(
        ladder_kernel,
        out_shape=jax.ShapeDtypeStruct((2, 1, rows, width), jnp.bfloat16),
        in_specs=[
            pl.BlockSpec(memory_space=pltpu.SMEM),
            pl.BlockSpec(memory_space=pl.ANY),
            pl.BlockSpec(memory_space=pl.ANY),
        ],
        out_specs=pl.BlockSpec(memory_space=pltpu.VMEM),
        scratch_shapes=[
            pltpu.VMEM((tiles, HALVES, rows, width), jnp.bfloat16),
            pltpu.VMEM((HALVES, width, width), jnp.bfloat16),
            pltpu.VMEM((tiles, width, rows), jnp.float32),
            pltpu.VMEM((4, width, rows), jnp.float32),
            pltpu.VMEM((2, width, rows), jnp.float32),
            pltpu.SemaphoreType.DMA,
            pltpu.SemaphoreType.DMA((HALVES,)),
            pltpu.SemaphoreType.DMA((tiles, HALVES * PARTS)),
            pltpu.SemaphoreType.DMA((tiles, HALVES * PARTS)),
            pltpu.SemaphoreType.DMA((tiles, HALVES * PARTS)),
            pltpu.SemaphoreType.DMA((tiles, HALVES * PARTS)),
            pltpu.SemaphoreType.DMA((4,)),
            pltpu.SemaphoreType.DMA((4,)),
            pltpu.SemaphoreType.DMA((2,)),
            pltpu.SemaphoreType.DMA((2,)),
        ],
        compiler_params=pltpu.CompilerParams(
            collective_id=0, has_side_effects=True, vmem_limit_bytes=56 * 2**20,
        ),
        cost_estimate=pl.CostEstimate(flops=flops, bytes_accessed=18 * 2**20, transcendentals=0),
    )(listed.astype(jnp.float32), amplitudes, integrals)


def body(amplitudes, integrals, triples):
    occ_local, cd_local, rows, width = amplitudes.shape
    ab_local = integrals.shape[0]
    gathered = lax.all_gather(amplitudes, "mem", axis=0, tiled=True)
    occ_tiles = gathered.shape[0]
    pairs = ab_local * cd_local
    codes = triples.reshape(-1)
    capacity = codes.shape[0]
    live = codes >= 0
    safe = jnp.maximum(codes, 0)
    occ_index = jnp.where(live, safe // pairs, occ_tiles)
    ab_index = safe % pairs // cd_local
    cd_index = safe % cd_local
    amp_flat = gathered.reshape(occ_tiles * cd_local, rows, width)
    int_flat = integrals.reshape(pairs, width, width)
    live_count = jnp.sum(live.astype(jnp.int32))
    empty = jnp.zeros((occ_tiles * ab_local, rows, width), jnp.float32)

    def one_triple(slot, total):
        place = jnp.minimum(slot, capacity - 1)
        occ = occ_index[place]
        outer = ab_index[place]
        inner = cd_index[place]
        left = lax.dynamic_index_in_dim(amp_flat, occ * cd_local + inner, 0, keepdims=False)
        right = lax.dynamic_index_in_dim(int_flat, outer * cd_local + inner, 0, keepdims=False)
        product = lax.dot_general(
            left, right, (((1,), (1,)), ((), ())), preferred_element_type=jnp.float32
        )
        target_row = (occ - 0) * ab_local + outer
        current = lax.dynamic_index_in_dim(total, target_row, 0, keepdims=False)
        return lax.dynamic_update_index_in_dim(total, current + product, target_row, 0)

    partial_value = lax.fori_loop(0, live_count, one_triple, empty)
    summed = lax.psum_scatter(
        partial_value.reshape(occ_tiles, ab_local, rows, width),
        "grp",
        scatter_dimension=0,
        tiled=True,
    )
    return summed.astype(jnp.bfloat16)


def solution(mesh):
    small = (mesh.shape["grp"], mesh.shape["mem"]) == (4, 8)
    return jax.shard_map(
        fused_body if small else body,
        mesh=mesh,
        in_specs=(P("mem", "grp", None, None), P("mem", "grp", None, None), P("grp", "mem", None)),
        out_specs=P("grp", "mem", None, None),
        check_vma=False,
    )
```

```python
import functools

import jax
import jax.numpy as jnp
from jax import lax
from jax.experimental import pallas as pl
from jax.experimental.pallas import tpu as pltpu
from jax.sharding import PartitionSpec as P

MESH = pl.DeviceIdType.MESH
LINE = 4
HALVES = 2
PARTS = 2

FIRST_SENDS = 6
MAIN_EVENTS = 114
EVENTS = (
    (
        8700960, 25183331, 33604131, 9965574, 67731618, 10228231, 67994246, 4196488, 67208304, 29630981,
        67471012, 4728976, 71404658, 30156309, 71667378, 6302868, 6169720, 47772185, 7418131, 73462810,
        32257565, 48812648, 7944473, 8270858, 74273803, 3676350, 3939080, 45748876, 75645216, 75645216,
        75645216, 75645216, 75645216, 75645216, 75645216, 75645216, 75645216, 75645216, 75645216,
    ),
    (
        27824168, 28086825, 35673642, 4201472, 29401120, 60919978, 3932938, 21250577, 52756593, 37361385,
        4728834, 29926434, 71426250, 5506704, 21775891, 53298291, 46801649, 6302726, 50393176, 38937842,
        6565383, 35189337, 72214209, 6830262, 50918490, 39989496, 23868957, 27300987, 48812619, 73790147,
        25205916, 74052638, 8176207, 74315454, 69325836, 61691917, 62392585, 42994432, 75629295,
    ),
    (
        29925424, 30188081, 29402162, 29664819, 5771408, 23096344, 54617208, 2499824, 14430743, 35713625,
        72213201, 5248150, 55096346, 39985394, 7088651, 55399515, 47325939, 7878656, 56148000, 48902392,
        8141313, 33604129, 73790167, 1049756, 50381858, 49938682, 9177603, 27283555, 42521129, 67499713,
        27808900, 67732486, 1889835, 67995302, 69308428, 52762637, 52960521, 45621002, 75634379,
    ),
    (
        23393368, 23901307, 7872664, 48816222, 4601080, 29670943, 37810808, 41563897, 65546258, 5515024,
        71694002, 7351444, 6172926, 66939933, 96537, 25428576, 67111040, 1360898, 918148, 1655907, 27267330,
        67980295, 35705353, 2756620, 36706922, 28055305, 69737642, 75586575, 75645216, 75645216, 75645216,
        75645216, 75645216, 75645216, 75645216, 75645216, 75645216, 75645216, 75645195,
    ),
)


def ladder_kernel(mask_ref, amp_ref, int_ref, out_ref, held, ints, part, near, far,
                  load_sem, ints_sem, get_sem, up_sem, down_sem, side_sem,
                  core_send, core_get, far_send, far_get):
    grp, mem = lax.axis_index("grp"), lax.axis_index("mem")
    x, core = grp // 2, grp % 2
    z, y = mem // 2, mem % 2
    place_z = z + x * (LINE - 1 - 2 * z)
    toward = 2 - 4 * x
    up, down, side = {"mem": mem + toward}, {"mem": mem - toward}, {"mem": z * 2 + 1 - y}
    twin = {"grp": x * 2 + 1 - core}
    across = {"grp": (1 - x) * 2 + core}
    width = ints.shape[1]
    rows = held.shape[2]

    load = pltpu.make_async_copy(amp_ref.at[0], held.at[mem], load_sem)
    load.start()
    fetch = [pltpu.make_async_copy(int_ref.at[0, h], ints.at[h], ints_sem.at[h]) for h in range(HALVES)]
    for copy in fetch:
        copy.start()

    barrier = pltpu.get_barrier_semaphore()
    for neighbour in (side, twin, across):
        pl.semaphore_signal(barrier, inc=1, device_id=neighbour, device_id_type=MESH)

    @pl.when(place_z < LINE - 1)
    def _():
        pl.semaphore_signal(barrier, inc=1, device_id=up, device_id_type=MESH)

    @pl.when(place_z > 0)
    def _():
        pl.semaphore_signal(barrier, inc=1, device_id=down, device_id_type=MESH)

    @pl.when((z > 0) & (z < LINE - 1))
    def _():
        pl.semaphore_wait(barrier, 5)

    @pl.when((z == 0) | (z == LINE - 1))
    def _():
        pl.semaphore_wait(barrier, 4)

    load.wait()

    share = rows // PARTS

    def push(tile, half, piece, sems, target):
        at = pl.ds(pl.multiple_of(piece * share, share), share)
        return pltpu.make_async_remote_copy(
            src_ref=held.at[tile, half, at], dst_ref=held.at[tile, half, at],
            send_sem=sems.at[tile, half * PARTS + piece], recv_sem=get_sem.at[tile, half * PARTS + piece],
            device_id=target, device_id_type=MESH,
        )

    words = []
    for choices in zip(*EVENTS):
        word = jnp.int32(choices[0])
        for i in range(1, LINE):
            word = jnp.where(place_z == i, choices[i], word)
        words.append(word)

    def event(step):
        word = words[0]
        for i in range(1, len(words)):
            word = jnp.where(step // 3 == i, words[i], word)
        third = step % 3
        code = word // jnp.where(third == 0, 1, jnp.where(third == 1, 512, 512 * 512)) % 512
        sz = code // 8 % 4
        sz = sz + x * (LINE - 1 - 2 * sz)
        other = code // 4 % 2
        tile = sz * 2 + y + other - 2 * y * other
        return code // 32, tile, code // 2 % 2, code % 2

    ways = ((up_sem, up), (down_sem, down), (side_sem, side))

    def to_twin(tile):
        place = tile // 4 * 2 + tile % 2
        return pltpu.make_async_remote_copy(
            src_ref=part.at[tile], dst_ref=near.at[place],
            send_sem=core_send.at[place], recv_sem=core_get.at[place],
            device_id=twin, device_id_type=MESH,
        )

    def to_across(tile):
        place = tile % 2
        return pltpu.make_async_remote_copy(
            src_ref=part.at[tile], dst_ref=far.at[place],
            send_sem=far_send.at[place], recv_sem=far_get.at[place],
            device_id=across, device_id_type=MESH,
        )

    def multiply(tile, half):
        scale = mask_ref[tile * 2 + half]

        def columns(n, inner):
            at = pl.ds(pl.multiple_of(n * 512, 512), 512)
            product = lax.dot_general(
                ints[half, at, :], held[tile, half], (((1,), (1,)), ((), ())),
                preferred_element_type=jnp.float32,
            )
            part[tile, at, :] += product * scale
            return inner

        lax.fori_loop(0, width // 512, columns, 0)

    def one_event(step, carry):
        kind, tile, half, piece = event(step)

        @pl.when(kind == 0)
        def _():
            push(tile, half, piece, side_sem, side).wait_recv()

        for i, (sems, target) in enumerate(ways):
            @pl.when(kind == 1 + i)
            def _():
                push(tile, half, piece, sems, target).start()

            @pl.when(kind == 6 + i)
            def _():
                push(tile, half, piece, sems, target).wait_send()

        @pl.when((kind == 4) | (kind == 5))
        def _():
            multiply(tile, half)

        mine = tile // 2 % 2 == core

        @pl.when((kind == 5) & jnp.logical_not(mine))
        def _():
            to_twin(tile).start()

        @pl.when((kind == 5) & mine & (tile // 4 != x))
        def _():
            to_twin(tile).wait_recv()
            part[tile] += near[tile // 4 * 2 + tile % 2]
            to_across(tile).start()

        return carry

    lax.fori_loop(0, FIRST_SENDS, one_event, 0)
    part[...] = jnp.zeros_like(part)
    for copy in fetch:
        copy.wait()

    lax.fori_loop(FIRST_SENDS, MAIN_EVENTS, one_event, 0)

    for k in range(2):
        tile = grp * 2 + k
        to_twin(tile).wait_recv()
        kept = part[tile] + near[x * 2 + k]
        to_across(tile).wait_recv()
        out_ref[k, 0] = (kept + far[k]).T.astype(out_ref.dtype)

    lax.fori_loop(MAIN_EVENTS, 3 * len(words), one_event, 0)
    for place in range(4):
        tile = place // 2 * 4 + (1 - core) * 2 + place % 2
        to_twin(tile).wait_send()
    for k in range(2):
        to_across((1 - x) * 4 + core * 2 + k).wait_send()


def fused_body(amplitudes, integrals, triples):
    rows, width = amplitudes.shape[2:]
    codes = triples.reshape(-1)
    tiles = 8
    listed = (codes[None, :] == jnp.arange(tiles * HALVES, dtype=jnp.int32)[:, None]).any(axis=1)
    flops = 2 * tiles * HALVES * rows * width * width
    return pl.pallas_call(
        ladder_kernel,
        out_shape=jax.ShapeDtypeStruct((2, 1, rows, width), jnp.bfloat16),
        in_specs=[
            pl.BlockSpec(memory_space=pltpu.SMEM),
            pl.BlockSpec(memory_space=pl.ANY),
            pl.BlockSpec(memory_space=pl.ANY),
        ],
        out_specs=pl.BlockSpec(memory_space=pltpu.VMEM),
        scratch_shapes=[
            pltpu.VMEM((tiles, HALVES, rows, width), jnp.bfloat16),
            pltpu.VMEM((HALVES, width, width), jnp.bfloat16),
            pltpu.VMEM((tiles, width, rows), jnp.float32),
            pltpu.VMEM((4, width, rows), jnp.float32),
            pltpu.VMEM((2, width, rows), jnp.float32),
            pltpu.SemaphoreType.DMA,
            pltpu.SemaphoreType.DMA((HALVES,)),
            pltpu.SemaphoreType.DMA((tiles, HALVES * PARTS)),
            pltpu.SemaphoreType.DMA((tiles, HALVES * PARTS)),
            pltpu.SemaphoreType.DMA((tiles, HALVES * PARTS)),
            pltpu.SemaphoreType.DMA((tiles, HALVES * PARTS)),
            pltpu.SemaphoreType.DMA((4,)),
            pltpu.SemaphoreType.DMA((4,)),
            pltpu.SemaphoreType.DMA((2,)),
            pltpu.SemaphoreType.DMA((2,)),
        ],
        compiler_params=pltpu.CompilerParams(
            collective_id=0, has_side_effects=True, vmem_limit_bytes=56 * 2**20,
        ),
        cost_estimate=pl.CostEstimate(flops=flops, bytes_accessed=18 * 2**20, transcendentals=0),
    )(listed.astype(jnp.float32), amplitudes, integrals)


def body(amplitudes, integrals, triples):
    occ_local, cd_local, rows, width = amplitudes.shape
    ab_local = integrals.shape[0]
    gathered = lax.all_gather(amplitudes, "mem", axis=0, tiled=True)
    occ_tiles = gathered.shape[0]
    pairs = ab_local * cd_local
    codes = triples.reshape(-1)
    capacity = codes.shape[0]
    live = codes >= 0
    safe = jnp.maximum(codes, 0)
    occ_index = jnp.where(live, safe // pairs, occ_tiles)
    ab_index = safe % pairs // cd_local
    cd_index = safe % cd_local
    amp_flat = gathered.reshape(occ_tiles * cd_local, rows, width)
    int_flat = integrals.reshape(pairs, width, width)
    live_count = jnp.sum(live.astype(jnp.int32))
    empty = jnp.zeros((occ_tiles * ab_local, rows, width), jnp.float32)

    def one_triple(slot, total):
        place = jnp.minimum(slot, capacity - 1)
        occ = occ_index[place]
        outer = ab_index[place]
        inner = cd_index[place]
        left = lax.dynamic_index_in_dim(amp_flat, occ * cd_local + inner, 0, keepdims=False)
        right = lax.dynamic_index_in_dim(int_flat, outer * cd_local + inner, 0, keepdims=False)
        product = lax.dot_general(
            left, right, (((1,), (1,)), ((), ())), preferred_element_type=jnp.float32
        )
        target_row = (occ - 0) * ab_local + outer
        current = lax.dynamic_index_in_dim(total, target_row, 0, keepdims=False)
        return lax.dynamic_update_index_in_dim(total, current + product, target_row, 0)

    partial_value = lax.fori_loop(0, live_count, one_triple, empty)
    summed = lax.psum_scatter(
        partial_value.reshape(occ_tiles, ab_local, rows, width),
        "grp",
        scatter_dimension=0,
        tiled=True,
    )
    return summed.astype(jnp.bfloat16)


def solution(mesh):
    small = (mesh.shape["grp"], mesh.shape["mem"]) == (4, 8)
    return jax.shard_map(
        fused_body if small else body,
        mesh=mesh,
        in_specs=(P("mem", "grp", None, None), P("mem", "grp", None, None), P("grp", "mem", None)),
        out_specs=P("grp", "mem", None, None),
        check_vma=False,
    )
```
